128 devices in a mesh: leaf: 128 (over y, x, z, core).
Axes of the slice: x: 4, y: 4, z: 4, core: 2. Of those that a mesh axis runs over, the one named last changes fastest.
Arguments:
- charges: bfloat16 [32768, 128, 128], P('leaf'), may hold values from -6 to 6
- basis_in: bfloat16 [32768, 64, 128], P('leaf'), may hold values from -0.5 to 0.5
- basis_out: bfloat16 [32768, 64, 128], P('leaf'), may hold values from -0.75 to 0.75
- transfer: bfloat16 [4096, 8, 64, 64], P('leaf'), may hold values from -0.375 to 0.375
- leaf_coupling: bfloat16 [16, 64, 64], replicated, may hold values from -0.25 to 0.25
- parent_coupling: bfloat16 [16, 64, 64], replicated, may hold values from -0.25 to 0.25
- leaf_sources: int32 [32768, 16], P('leaf'), may hold values from 0 to 511, as said below
- leaf_counts: int32 [32768], P('leaf'), may hold values from 2 to 16
- leaf_sends: int32 [128, 2, 128], replicated, may hold values from 0 to 255, as said below
- parent_sources: int32 [4096, 16], P('leaf'), may hold values from 0 to 159, as said below
- parent_counts: int32 [4096], P('leaf'), may hold values from 12 to 16
- parent_sends: int32 [128, 128], replicated, may hold values from 0 to 31
Outputs:
- potential: bfloat16 [32768, 128, 128], P('leaf')
The draws below stay inside these ranges and needn't reach their ends.
Inputs may be any that keep to these rules, and one draw needn't show every extreme that they name: `leaf_sources`: every row of a device's leaf pool is read by some used slot of that device's leaf lists. `leaf_sends`: the 128 leaves offered in one direction are distinct. `parent_sources`: every row of a device's parent pool is read by some used slot of that device's parent lists.
All inputs are finite; a program needn't handle non-finite values.
Results may differ from the reference program's by a relative error of at most 0.007.
Values may be sent and summed in bfloat16 or wider, within the bound.
No kernel may reach another device: no remote copies, remote signals or barrier semaphores. Data moves between devices by JAX's collectives and lax.ppermute only.
A program may use at most 256 MiB of HBM per device.

```python
import jax
import jax.numpy as jnp
from jax import lax

K = 64
R = 128
PTS = 128
LIST0 = 16
LIST1 = 16
LEAF_DEV = 256
NODE1 = 32
SIDE = 128
LEAVES = 32768
NODES1 = 4096
N_LEAF = 128


def pool_columns(device_key, pool_size, targets, list_width):
    leading_cols = -(-pool_size // targets)
    spare = leading_cols * targets - pool_size
    order = jax.random.permutation(jax.random.fold_in(device_key, 1), pool_size).astype(jnp.int32)
    filler = jax.random.randint(jax.random.fold_in(device_key, 2), (spare,), 0, pool_size, dtype=jnp.int32)
    leading = jnp.concatenate([order, filler]).reshape(leading_cols, targets).T
    trailing = jax.random.randint(jax.random.fold_in(device_key, 3), (targets, list_width - leading_cols), 0, pool_size, dtype=jnp.int32)
    return jnp.concatenate([leading, trailing], 1)


def draw_leaf_sources(key, part):
    key = jax.random.fold_in(key, 11)

    def one_device(device_key):
        return pool_columns(device_key, LEAF_DEV + 2 * SIDE, LEAF_DEV, LIST0)
    return jax.vmap(one_device)(jax.random.split(key, N_LEAF)).reshape(LEAVES, LIST0)


def draw_parent_sources(key, part):
    key = jax.random.fold_in(key, 14)

    def one_device(device_key):
        return pool_columns(device_key, NODE1 + N_LEAF, NODE1, LIST1)
    return jax.vmap(one_device)(jax.random.split(key, N_LEAF)).reshape(NODES1, LIST1)


def draw_leaf_counts(key, part):
    key = jax.random.fold_in(key, 12)
    tops = jax.random.randint(jax.random.fold_in(key, 1), (N_LEAF, 1), LIST0 // 2, LIST0 + 1, dtype=jnp.int32)
    first = jax.random.randint(jax.random.fold_in(key, 2), (N_LEAF, LEAF_DEV), 0, 1 << 20, dtype=jnp.int32) % (tops - 1)
    second = jax.random.randint(jax.random.fold_in(key, 3), (N_LEAF, LEAF_DEV), 0, 1 << 20, dtype=jnp.int32) % (tops - 1)
    counts = (2 + jnp.maximum(first, second)).reshape(LEAVES)
    chosen = jax.random.randint(jax.random.fold_in(key, 4), (), 0, LEAVES, dtype=jnp.int32)
    positions = jnp.arange(LEAVES, dtype=jnp.int32)
    counts = jnp.where(positions == chosen, LIST0, counts)
    counts = jnp.where(positions == (chosen + 1) % LEAVES, 2, counts)
    return counts.astype(jnp.int32)


def draw_parent_counts(key, part):
    key = jax.random.fold_in(key, 15)
    counts = jax.random.randint(jax.random.fold_in(key, 1), (NODES1,), LIST1 - LIST1 // 4, LIST1 + 1, dtype=jnp.int32)
    chosen = jax.random.randint(jax.random.fold_in(key, 2), (), 0, NODES1, dtype=jnp.int32)
    positions = jnp.arange(NODES1, dtype=jnp.int32)
    counts = jnp.where(positions == chosen, LIST1, counts)
    counts = jnp.where(positions == (chosen + 1) % NODES1, LIST1 - LIST1 // 4, counts)
    return counts.astype(jnp.int32)


def draw_leaf_sends(key, part):
    key = jax.random.fold_in(key, 13)

    def one_row(row_key):
        return jax.random.permutation(row_key, LEAF_DEV)[:SIDE].astype(jnp.int32)
    return jax.vmap(one_row)(jax.random.split(key, 2 * N_LEAF)).reshape(N_LEAF, 2, SIDE)


def draw_parent_sends(key, part):
    key = jax.random.fold_in(key, 16)
    return jax.random.randint(key, (N_LEAF, N_LEAF), 0, NODE1, dtype=jnp.int32)


def block_scale(rng, extent, cuts, least, high):
    def one(axis_at, shards_of):
        draws = jax.random.uniform(jax.random.fold_in(jax.random.fold_in(rng, 6), axis_at), (shards_of,), jnp.float32, least / len(cuts), high / len(cuts))
        return jnp.repeat(jnp.exp(draws), extent[axis_at] // shards_of).reshape((-1,) + (1,) * (len(extent) - axis_at - 1))

    factor_of = one(*cuts[0])
    for cut in cuts[1:]:
        factor_of = factor_of * one(*cut)
    return factor_of


def noise(own_key, dims, width, limit, cuts=(), kind=jnp.bfloat16):
    gain = block_scale(own_key, dims, cuts, -0.22, 0.18) if cuts else 1.0
    values = jax.random.normal(own_key, dims, jnp.float32) * width * gain
    return jnp.minimum(jnp.maximum(values, -limit), limit).astype(kind)


def setup_inputs(seed: int = 0) -> dict:
    key_list = jax.random.split(jax.random.key(seed), 13)
    return {
        "charges": noise(key_list[0], (LEAVES, PTS, R), 1.0, 6.0, ((0, 128),)),
        "basis_in": noise(key_list[1], (LEAVES, K, PTS), PTS ** -0.5, 0.5, ((0, 128),)),
        "basis_out": noise(key_list[2], (LEAVES, K, PTS), K ** -0.5, 0.75, ((0, 128),)),
        "transfer": noise(key_list[3], (NODES1, 8, K, K), (4 * K) ** -0.5, 0.375, ((0, 128),)),
        "leaf_coupling": noise(key_list[4], (LIST0, K, K), (K * LIST0 // 2) ** -0.5, 0.25),
        "parent_coupling": noise(key_list[5], (LIST1, K, K), (K * LIST1 // 2) ** -0.5, 0.25),
        "leaf_sources": draw_leaf_sources(jax.random.fold_in(key_list[12], 71), 0),
        "leaf_counts": draw_leaf_counts(jax.random.fold_in(key_list[12], 71), 0),
        "leaf_sends": draw_leaf_sends(jax.random.fold_in(key_list[12], 71), 0),
        "parent_sources": draw_parent_sources(jax.random.fold_in(key_list[12], 71), 0),
        "parent_counts": draw_parent_counts(jax.random.fold_in(key_list[12], 71), 0),
        "parent_sends": draw_parent_sends(jax.random.fold_in(key_list[12], 71), 0),
    }


def split_devices(array):
    return array.reshape((N_LEAF, array.shape[0] // N_LEAF) + array.shape[1:])


def pooled_product(pool_rows, sources, counts, coupling):
    list_width = sources.shape[1]
    valid_mask = jnp.arange(list_width, dtype=jnp.int32)[None, :] < counts[:, None]
    picked = jnp.where(valid_mask[:, :, None, None], pool_rows[sources], jnp.zeros((), pool_rows.dtype))
    return jnp.einsum("jab,tjbr->tar", coupling.astype(jnp.float32), picked.astype(jnp.float32))


def reference(charges, basis_in, basis_out, transfer, leaf_coupling, parent_coupling, leaf_sources, leaf_counts, leaf_sends, parent_sources, parent_counts, parent_sends):
    def upward(pieces):
        densities, columns, parents = pieces
        leaf_up = jnp.einsum("nkp,npr->nkr", columns.astype(jnp.float32), densities.astype(jnp.float32)).astype(jnp.bfloat16)
        leaf_up = lax.optimization_barrier(leaf_up)
        grouped = leaf_up.astype(jnp.float32).reshape(NODE1, 8, K, R)
        parent_up = jnp.einsum("pcab,pcar->pbr", parents.astype(jnp.float32), grouped).astype(jnp.bfloat16)
        return leaf_up, parent_up

    up_leaf, up_parent = lax.map(upward, (split_devices(charges), split_devices(basis_in), split_devices(transfer)))
    sources_leaf = split_devices(leaf_sources)
    counts_leaf = split_devices(leaf_counts)
    sources_parent = split_devices(parent_sources)
    counts_parent = split_devices(parent_counts)
    rows_out = split_devices(basis_out)
    transfers = split_devices(transfer)
    device_ids = jnp.arange(N_LEAF, dtype=jnp.int32)

    def per_device(device):
        left_dev = jnp.maximum(device - 1, 0)
        right_dev = jnp.minimum(device + 1, N_LEAF - 1)
        from_left = up_leaf[left_dev][leaf_sends[left_dev, 1]]
        from_left = jnp.where(device > 0, from_left, jnp.zeros_like(from_left))
        from_right = up_leaf[right_dev][leaf_sends[right_dev, 0]]
        from_right = jnp.where(device < N_LEAF - 1, from_right, jnp.zeros_like(from_right))
        leaf_pool = jnp.concatenate([up_leaf[device], from_left, from_right], 0)
        leaf_field = pooled_product(leaf_pool, sources_leaf[device], counts_leaf[device], leaf_coupling)
        arrived = up_parent[device_ids, parent_sends[:, device]]
        parent_pool = jnp.concatenate([up_parent[device], arrived], 0)
        parent_field = pooled_product(parent_pool, sources_parent[device], counts_parent[device], parent_coupling)
        parent_down = lax.optimization_barrier(parent_field.astype(jnp.bfloat16))
        pushed = jnp.einsum("pcab,pbr->pcar", transfers[device].astype(jnp.float32), parent_down.astype(jnp.float32)).reshape(LEAF_DEV, K, R)
        leaf_total = lax.optimization_barrier((leaf_field + pushed).astype(jnp.bfloat16))
        return jnp.einsum("nkp,nkr->npr", rows_out[device].astype(jnp.float32), leaf_total.astype(jnp.float32)).astype(jnp.bfloat16)

    return lax.map(per_device, device_ids).reshape(LEAVES, PTS, R)
```

```python
import functools

import jax
import jax.numpy as jnp
from jax import lax
from jax.experimental import pallas as pl
from jax.experimental.pallas import tpu as pltpu
from jax.sharding import PartitionSpec as P

MIB = 1 << 20
F32 = jnp.float32
BF16 = jnp.bfloat16


def params(mib):
    return pltpu.CompilerParams(
        vmem_limit_bytes=mib * MIB, dimension_semantics=("arbitrary",)
    )


def up_kernel(
    own_ref,
    leaf_sends_ref,
    parent_sends_ref,
    charges_ref,
    basis_ref,
    transfer_ref,
    up_leaf_ref,
    up_parent_ref,
    low_ref,
    high_ref,
    parents_ref,
    all_leaf,
):
    step = pl.program_id(0)
    steps = pl.num_programs(0)
    leaves = charges_ref.shape[0]
    rank, rhs = up_leaf_ref.shape[1:]
    for p in range(leaves // 8):
        for c in range(8):
            n = 8 * p + c
            up = jnp.dot(basis_ref[n], charges_ref[n], preferred_element_type=F32).astype(BF16)
            up_leaf_ref[n] = up
            all_leaf[step * leaves + n] = up
        stacked = transfer_ref[p].reshape(8 * rank, rank)
        below = up_leaf_ref[8 * p : 8 * p + 8].reshape(8 * rank, rhs)
        up_parent_ref[step * (leaves // 8) + p] = lax.dot_general(
            stacked, below, (((0,), (0,)), ((), ())), preferred_element_type=F32
        ).astype(BF16)

    @pl.when(step == steps - 1)
    def _():
        mine = lax.rem(own_ref[0], parent_sends_ref.shape[0])

        @pl.loop(0, low_ref.shape[0], unroll=4)
        def _(i):
            low_ref[i] = all_leaf[leaf_sends_ref[0, 0, i]]
            high_ref[i] = all_leaf[leaf_sends_ref[0, 1, i]]

        @pl.loop(0, parents_ref.shape[0], unroll=4)
        def _(i):
            parents_ref[i] = up_parent_ref[parent_sends_ref[mine, i]]


def upward(own, leaf_sends, parent_sends, charges, basis_in, transfer):
    per_dev, points, rhs = charges.shape
    rank = basis_in.shape[1]
    parents = transfer.shape[0]
    side = leaf_sends.shape[2]
    count_dev = parent_sends.shape[0]
    steps = 8
    lb = per_dev // steps
    whole = lambda i, own: (0, 0, 0)
    return pl.pallas_call(
        up_kernel,
        grid_spec=pltpu.PrefetchScalarGridSpec(
            num_scalar_prefetch=1,
            grid=(steps,),
            in_specs=[
                pl.BlockSpec((1, 2, side), lambda i, own: (own[0], 0, 0), memory_space=pltpu.SMEM),
                pl.BlockSpec((8, count_dev), lambda i, own: (own[0] // 8, 0), memory_space=pltpu.SMEM),
                pl.BlockSpec((lb, points, rhs), lambda i, own: (i, 0, 0)),
                pl.BlockSpec((lb, rank, points), lambda i, own: (i, 0, 0)),
                pl.BlockSpec((lb // 8, 8, rank, rank), lambda i, own: (i, 0, 0, 0)),
            ],
            out_specs=[
                pl.BlockSpec((lb, rank, rhs), lambda i, own: (i, 0, 0)),
                pl.BlockSpec((parents, rank, rhs), whole),
                pl.BlockSpec((side, rank, rhs), whole),
                pl.BlockSpec((side, rank, rhs), whole),
                pl.BlockSpec((count_dev, rank, rhs), whole),
            ],
            scratch_shapes=[pltpu.VMEM((per_dev, rank, rhs), BF16)],
        ),
        out_shape=[
            jax.ShapeDtypeStruct((per_dev, rank, rhs), BF16),
            jax.ShapeDtypeStruct((parents, rank, rhs), BF16),
            jax.ShapeDtypeStruct((side, rank, rhs), BF16),
            jax.ShapeDtypeStruct((side, rank, rhs), BF16),
            jax.ShapeDtypeStruct((count_dev, rank, rhs), BF16),
        ],
        compiler_params=params(48),
        name="upward",
    )(own, leaf_sends, parent_sends, charges, basis_in, transfer)


def gathered(pool, sources, counts, row, zero_row):
    width = sources.shape[1]
    count = counts[row]
    tiles = [pool[jnp.where(j < count, sources[row, j], zero_row)] for j in range(width)]
    return jnp.concatenate(tiles, axis=0)


def leaf_kernel(
    sources_ref,
    counts_ref,
    stacked_ref,
    own_ref,
    left_ref,
    right_ref,
    field_ref,
    pool,
    sems,
):
    step = pl.program_id(0)
    block = field_ref.shape[0]
    own_rows, rank, rhs = own_ref.shape
    left_rows = left_ref.shape[0]
    right_rows = right_ref.shape[0]
    zero_row = own_rows + left_rows + right_rows

    @pl.when(step == 0)
    def _():
        copies = [
            pltpu.make_async_copy(own_ref, pool.at[pl.ds(0, own_rows)], sems.at[0]),
            pltpu.make_async_copy(left_ref, pool.at[pl.ds(own_rows, left_rows)], sems.at[1]),
            pltpu.make_async_copy(right_ref, pool.at[pl.ds(own_rows + left_rows, right_rows)], sems.at[2]),
        ]
        for copy in copies:
            copy.start()
        pool[zero_row] = jnp.zeros((rank, rhs), BF16)
        for copy in copies:
            copy.wait()

    @pl.loop(0, block // 2)
    def _(i):
        row = step * block + 2 * i
        pair = jnp.concatenate(
            [
                gathered(pool, sources_ref, counts_ref, row, zero_row),
                gathered(pool, sources_ref, counts_ref, row + 1, zero_row),
            ],
            axis=1,
        )
        field = jnp.dot(stacked_ref[...], pair, preferred_element_type=F32)
        field_ref[2 * i] = field[:, :rhs].astype(field_ref.dtype)
        field_ref[2 * i + 1] = field[:, rhs:].astype(field_ref.dtype)


def leaf_lists(sources, counts, stacked, own, left, right):
    per_dev, rank, rhs = own.shape
    rows = own.shape[0] + left.shape[0] + right.shape[0]
    steps = 8
    block = per_dev // steps
    return pl.pallas_call(
        leaf_kernel,
        grid=(steps,),
        in_specs=[
            pl.BlockSpec(memory_space=pltpu.SMEM),
            pl.BlockSpec(memory_space=pltpu.SMEM),
            pl.BlockSpec(stacked.shape, lambda i: (0, 0)),
            pl.BlockSpec(memory_space=pl.ANY),
            pl.BlockSpec(memory_space=pl.ANY),
            pl.BlockSpec(memory_space=pl.ANY),
        ],
        out_specs=pl.BlockSpec((block, rank, rhs), lambda i: (i, 0, 0)),
        out_shape=jax.ShapeDtypeStruct((per_dev, rank, rhs), F32),
        scratch_shapes=[
            pltpu.VMEM((rows + 1, rank, rhs), BF16),
            pltpu.SemaphoreType.DMA((3,)),
        ],
        compiler_params=params(32),
        name="leaf_lists",
    )(sources, counts, stacked, own, left, right)


def down_kernel(
    sources_ref,
    counts_ref,
    stacked_ref,
    own_ref,
    arrived_ref,
    transfer_ref,
    field_ref,
    basis_ref,
    potential_ref,
    pool,
    sems,
):
    step = pl.program_id(0)
    block = transfer_ref.shape[0]
    own_rows, rank, rhs = own_ref.shape
    arrived_rows = arrived_ref.shape[0]
    zero_row = own_rows + arrived_rows

    @pl.when(step == 0)
    def _():
        copies = [
            pltpu.make_async_copy(own_ref, pool.at[pl.ds(0, own_rows)], sems.at[0]),
            pltpu.make_async_copy(arrived_ref, pool.at[pl.ds(own_rows, arrived_rows)], sems.at[1]),
        ]
        for copy in copies:
            copy.start()
        pool[zero_row] = jnp.zeros((rank, rhs), BF16)
        for copy in copies:
            copy.wait()

    for i in range(block // 2):
        row = step * block + 2 * i
        pair = jnp.concatenate(
            [
                gathered(pool, sources_ref, counts_ref, row, zero_row),
                gathered(pool, sources_ref, counts_ref, row + 1, zero_row),
            ],
            axis=1,
        )
        down = jnp.dot(stacked_ref[...], pair, preferred_element_type=F32).astype(BF16)
        for k in range(2):
            p = 2 * i + k
            pushed = jnp.dot(
                transfer_ref[p].reshape(8 * rank, rank),
                down[:, k * rhs : (k + 1) * rhs],
                preferred_element_type=F32,
            )
            for c in range(8):
                n = 8 * p + c
                total = (field_ref[n] + pushed[c * rank : (c + 1) * rank]).astype(BF16)
                potential_ref[n] = lax.dot_general(
                    basis_ref[n], total, (((0,), (0,)), ((), ())), preferred_element_type=F32
                ).astype(BF16)


def downward(sources, counts, stacked, own, arrived, transfer, field, basis_out):
    parents, rank, rhs = own.shape
    per_dev, _, points = basis_out.shape
    rows = own.shape[0] + arrived.shape[0]
    steps = 8
    block = parents // steps
    return pl.pallas_call(
        down_kernel,
        grid=(steps,),
        in_specs=[
            pl.BlockSpec(memory_space=pltpu.SMEM),
            pl.BlockSpec(memory_space=pltpu.SMEM),
            pl.BlockSpec(stacked.shape, lambda i: (0, 0)),
            pl.BlockSpec(memory_space=pl.ANY),
            pl.BlockSpec(memory_space=pl.ANY),
            pl.BlockSpec((block, 8, rank, rank), lambda i: (i, 0, 0, 0)),
            pl.BlockSpec((8 * block, rank, rhs), lambda i: (i, 0, 0)),
            pl.BlockSpec((8 * block, rank, points), lambda i: (i, 0, 0)),
        ],
        out_specs=pl.BlockSpec((8 * block, points, rhs), lambda i: (i, 0, 0)),
        out_shape=jax.ShapeDtypeStruct((per_dev, points, rhs), BF16),
        scratch_shapes=[
            pltpu.VMEM((rows + 1, rank, rhs), BF16),
            pltpu.SemaphoreType.DMA((2,)),
        ],
        compiler_params=params(32),
        name="downward",
    )(sources, counts, stacked, own, arrived, transfer, field, basis_out)


def side_by_side(coupling):
    width, rank, inner = coupling.shape
    return jnp.transpose(coupling, (1, 0, 2)).reshape(rank, width * inner)


def shards(
    charges,
    basis_in,
    basis_out,
    transfer,
    leaf_coupling,
    parent_coupling,
    leaf_sources,
    leaf_counts,
    leaf_sends,
    parent_sources,
    parent_counts,
    parent_sends,
):
    size = lax.axis_size("leaf")
    own = lax.axis_index("leaf").astype(jnp.int32).reshape(1)
    up = [(i, i + 1) for i in range(size - 1)]
    down = [(j, i) for i, j in up]
    up_leaf, up_parent, low, high, offered = upward(
        own, leaf_sends, parent_sends, charges, basis_in, transfer
    )
    from_left = lax.ppermute(high, "leaf", up)
    from_right = lax.ppermute(low, "leaf", down)
    arrived = lax.all_to_all(offered, "leaf", split_axis=0, concat_axis=0, tiled=True)
    field = leaf_lists(
        leaf_sources, leaf_counts, side_by_side(leaf_coupling), up_leaf, from_left, from_right
    )
    return downward(
        parent_sources,
        parent_counts,
        side_by_side(parent_coupling),
        up_parent,
        arrived,
        transfer,
        field,
        basis_out,
    )


def solution(mesh):
    return jax.shard_map(
        shards,
        mesh=mesh,
        in_specs=(
            P("leaf", None, None),
            P("leaf", None, None),
            P("leaf", None, None),
            P("leaf", None, None, None),
            P(),
            P(),
            P("leaf", None),
            P("leaf"),
            P(),
            P("leaf", None),
            P("leaf"),
            P(),
        ),
        out_specs=P("leaf", None, None),
        check_vma=False,
    )
```

```python
import jax
import jax.numpy as jnp
from jax import lax
from jax.experimental import pallas as pl
from jax.experimental.pallas import tpu as pltpu
from jax.sharding import PartitionSpec as P

MIB = 1 << 20
F32 = jnp.float32
BF16 = jnp.bfloat16

IN_VMEM = pl.BlockSpec(memory_space=pltpu.VMEM)
IN_SMEM = pl.BlockSpec(memory_space=pltpu.SMEM)
IN_HBM = pl.BlockSpec(memory_space=pltpu.HBM)


def params(mib):
    return pltpu.CompilerParams(vmem_limit_bytes=mib * MIB)


def cost(flops, moved):
    return pl.CostEstimate(flops=flops, bytes_accessed=moved, transcendentals=0)


def hbm(x):
    return pltpu.with_memory_space_constraint(x, pltpu.HBM)


def vmem(x):
    return pltpu.with_memory_space_constraint(x, pltpu.VMEM)


def first_rows_dot(a, b):
    return lax.dot_general(a, b, (((0,), (0,)), ((), ())), preferred_element_type=F32)


def leaves_kernel(
    own_ref, sends_ref, charges_hbm, basis_hbm, up_ref, low_ref, high_ref,
    charges, basis, sends, sems, send_sem,
):
    chunks = sems.shape[1]
    rows = charges.shape[0] // chunks

    def part(k, which):
        at = pl.ds(k * rows, rows)
        source, target = ((charges_hbm, charges), (basis_hbm, basis))[which]
        return pltpu.make_async_copy(source.at[at], target.at[at], sems.at[which, k])

    listing = pltpu.make_async_copy(sends_ref.at[own_ref[0]], sends, send_sem)
    for k in range(chunks):
        part(k, 0).start()
        part(k, 1).start()
    listing.start()
    for k in range(chunks):
        part(k, 0).wait()
        part(k, 1).wait()

        @pl.loop(0, rows // UP_LEAVES)
        def _(i):
            for c in range(UP_LEAVES):
                n = k * rows + UP_LEAVES * i + c
                up_ref[n] = jnp.dot(basis[n], charges[n], preferred_element_type=F32).astype(BF16)

    listing.wait()

    @pl.loop(0, low_ref.shape[0] // 4)
    def _(i):
        for c in range(4):
            low_ref[4 * i + c] = up_ref[sends[0, 4 * i + c]]
            high_ref[4 * i + c] = up_ref[sends[1, 4 * i + c]]


UP_LEAVES = 32


def leaf_coefficients(own, leaf_sends, charges, basis_in):
    per_dev, points, rhs = charges.shape
    rank = basis_in.shape[1]
    side = leaf_sends.shape[2]
    chunks = 8
    return pl.pallas_call(
        leaves_kernel,
        in_specs=[IN_SMEM, IN_HBM, IN_HBM, IN_HBM],
        out_specs=[IN_VMEM] * 3,
        out_shape=[
            pltpu.VMEM((per_dev, rank, rhs), BF16),
            pltpu.VMEM((side, rank, rhs), BF16),
            pltpu.VMEM((side, rank, rhs), BF16),
        ],
        scratch_shapes=[
            pltpu.VMEM((per_dev, points, rhs), BF16),
            pltpu.VMEM((per_dev, rank, points), BF16),
            pltpu.SMEM((2, side), jnp.int32),
            pltpu.SemaphoreType.DMA((2, chunks)),
            pltpu.SemaphoreType.DMA,
        ],
        compiler_params=params(16),
        cost_estimate=cost(2 * per_dev * rank * points * rhs, 20 * MIB),
        name="leaf_coefficients",
    )(own, hbm(leaf_sends), hbm(charges), hbm(basis_in))


def parents_kernel(
    own_ref, sends_ref, transfer_hbm, basis_hbm, leaf_ref, up_ref, offered_hbm, joined_hbm,
    transfer, basis, offered, joined, sends, sems, out_sems, send_sem, offer_sem,
):
    chunks = sems.shape[1]
    parents, _, rank, _ = transfer.shape
    rhs = leaf_ref.shape[2]
    rows = parents // chunks

    def part(k, which):
        if which:
            at = pl.ds(8 * k * rows, 8 * rows)
            return pltpu.make_async_copy(basis_hbm.at[at], basis.at[at], sems.at[1, k])
        at = pl.ds(k * rows, rows)
        return pltpu.make_async_copy(transfer_hbm.at[at], transfer.at[at], sems.at[0, k])

    def result(k):
        at = pl.ds(8 * k * rows, 8 * rows)
        return pltpu.make_async_copy(joined.at[at], joined_hbm.at[at], out_sems.at[k])

    own = own_ref[0]
    first = pl.multiple_of((own // 8) * 8, 8)
    listing = pltpu.make_async_copy(sends_ref.at[pl.ds(first, 8)], sends, send_sem)
    for k in range(chunks):
        part(k, 0).start()
    listing.start()
    for k in range(chunks):
        part(k, 1).start()
    for k in range(chunks):
        part(k, 0).wait()

        @pl.loop(0, rows // 4)
        def _(i):
            for c in range(4):
                p = k * rows + 4 * i + c
                below = leaf_ref[pl.ds(8 * p, 8)].reshape(8 * rank, rhs)
                up_ref[p] = first_rows_dot(transfer[p].reshape(8 * rank, rank), below).astype(BF16)

    listing.wait()
    row = lax.rem(own, 8)

    @pl.loop(0, offered.shape[0] // 8)
    def _(i):
        for c in range(8):
            offered[8 * i + c] = up_ref[sends[row, 8 * i + c]]

    offer = pltpu.make_async_copy(offered, offered_hbm, offer_sem)
    offer.start()
    for k in range(chunks):
        part(k, 1).wait()

        @pl.loop(0, rows)
        def _(i):
            p = k * rows + i
            for c in range(8):
                n = 8 * p + c
                pushed = first_rows_dot(transfer[p, c], basis[n]).astype(BF16)
                joined[n] = jnp.concatenate([basis[n], pushed], axis=0).T

        result(k).start()
    offer.wait()
    for k in range(chunks):
        result(k).wait()


def parent_coefficients(own, parent_sends, transfer, basis_out, up_leaf):
    parents, _, rank, _ = transfer.shape
    per_dev, _, points = basis_out.shape
    rhs = up_leaf.shape[2]
    count_dev = parent_sends.shape[0]
    chunks = 4
    return pl.pallas_call(
        parents_kernel,
        in_specs=[IN_SMEM, IN_HBM, IN_HBM, IN_HBM, IN_VMEM],
        out_specs=[IN_VMEM, IN_HBM, IN_HBM],
        out_shape=[
            pltpu.VMEM((parents, rank, rhs), BF16),
            pltpu.HBM((count_dev, rank, rhs), BF16),
            pltpu.HBM((per_dev, points, 2 * rank), BF16),
        ],
        scratch_shapes=[
            pltpu.VMEM(transfer.shape, BF16),
            pltpu.VMEM(basis_out.shape, BF16),
            pltpu.VMEM((count_dev, rank, rhs), BF16),
            pltpu.VMEM((per_dev, points, 2 * rank), BF16),
            pltpu.SMEM((8, count_dev), jnp.int32),
            pltpu.SemaphoreType.DMA((2, chunks)),
            pltpu.SemaphoreType.DMA((chunks,)),
            pltpu.SemaphoreType.DMA,
            pltpu.SemaphoreType.DMA,
        ],
        compiler_params=params(24),
        cost_estimate=cost(32 * parents * rank * rank * rhs, 20 * MIB),
        name="parent_coefficients",
    )(own, hbm(parent_sends), hbm(transfer), hbm(basis_out), vmem(up_leaf))


def list_fields(sources_ref, stacked, pool, first, count):
    width = sources_ref.shape[0]
    tiles = [
        jnp.concatenate([pool[sources_ref[j, first + q]] for j in range(width)], axis=0)
        for q in range(count)
    ]
    return jnp.dot(stacked, jnp.concatenate(tiles, axis=1), preferred_element_type=F32)


def fill(pool, *parts):
    first = 0
    for part in parts:
        rows = part.shape[0]

        @pl.loop(0, rows // 8)
        def _(i):
            for c in range(8):
                pool[first + 8 * i + c] = part[8 * i + c]

        first += rows
    pool[first] = jnp.zeros(pool.shape[1:], pool.dtype)


def lists_kernel(sources_ref, stacked_ref, own_ref, left_ref, right_ref, field_hbm, pool, field, sems):
    chunks = sems.shape[0]
    own_rows, _, rhs = own_ref.shape
    rows = own_rows // chunks
    fill(pool, own_ref, left_ref, right_ref)

    def result(k):
        at = pl.ds(k * rows, rows)
        return pltpu.make_async_copy(field.at[at], field_hbm.at[at], sems.at[k])

    for k in range(chunks):

        @pl.loop(0, rows // LISTS)
        def _(i):
            first = k * rows + LISTS * i
            lists = list_fields(sources_ref, stacked_ref[...], pool, first, LISTS)
            for q in range(LISTS):
                field[first + q] = lists[:, q * rhs : (q + 1) * rhs].astype(BF16)

        result(k).start()
    for k in range(chunks):
        result(k).wait()


LISTS = 8


def leaf_lists(sources, stacked, own, left, right):
    per_dev, rank, rhs = own.shape
    rows = own.shape[0] + left.shape[0] + right.shape[0]
    return pl.pallas_call(
        lists_kernel,
        in_specs=[IN_SMEM, IN_VMEM, IN_VMEM, IN_VMEM, IN_VMEM],
        out_specs=IN_HBM,
        out_shape=pltpu.HBM((per_dev, rank, rhs), BF16),
        scratch_shapes=[
            pltpu.VMEM((rows + 1, rank, rhs), BF16),
            pltpu.VMEM((per_dev, rank, rhs), BF16),
            pltpu.SemaphoreType.DMA((4,)),
        ],
        compiler_params=params(20),
        cost_estimate=cost(2 * per_dev * sources.shape[0] * rank * rank * rhs, 12 * MIB),
        name="leaf_lists",
    )(sources, stacked, vmem(own), vmem(left), vmem(right))


def down_kernel(
    sources_ref, stacked_ref, own_ref, arrived_ref, field_hbm, joined_hbm, potential_hbm,
    pool, down, field, joined, potential, sems, out_sems,
):
    chunks = out_sems.shape[0]
    parents, _, rhs = own_ref.shape
    rows = joined.shape[0] // chunks

    def part(k, which):
        at = pl.ds(k * rows, rows)
        source, target = ((field_hbm, field), (joined_hbm, joined))[which]
        return pltpu.make_async_copy(source.at[at], target.at[at], sems.at[which, k])

    def result(k):
        at = pl.ds(k * rows, rows)
        return pltpu.make_async_copy(potential.at[at], potential_hbm.at[at], out_sems.at[k])

    for k in range(chunks):
        part(k, 0).start()
        part(k, 1).start()
    fill(pool, own_ref, arrived_ref)

    @pl.loop(0, parents // DOWN_LISTS)
    def _(i):
        lists = list_fields(sources_ref, stacked_ref[...], pool, DOWN_LISTS * i, DOWN_LISTS)
        for q in range(DOWN_LISTS):
            down[DOWN_LISTS * i + q] = lists[:, q * rhs : (q + 1) * rhs].astype(BF16)

    for k in range(chunks):
        part(k, 0).wait()
        part(k, 1).wait()

        @pl.loop(0, rows // (8 * DOWN_PARENTS))
        def _(i):
            for q in range(DOWN_PARENTS):
                p = k * (rows // 8) + DOWN_PARENTS * i + q
                for c in range(8):
                    n = 8 * p + c
                    both = jnp.concatenate([field[n], down[p]], axis=0)
                    potential[n] = jnp.dot(joined[n], both, preferred_element_type=F32).astype(BF16)

        result(k).start()
    for k in range(chunks):
        result(k).wait()


DOWN_LISTS = 8
DOWN_PARENTS = 4
DOWN_CHUNKS = 8


def downward(sources, stacked, own, arrived, field, joined):
    parents, rank, rhs = own.shape
    per_dev, points, _ = joined.shape
    rows = own.shape[0] + arrived.shape[0]
    chunks = DOWN_CHUNKS
    return pl.pallas_call(
        down_kernel,
        in_specs=[IN_SMEM, IN_VMEM, IN_VMEM, IN_VMEM, IN_HBM, IN_HBM],
        out_specs=IN_HBM,
        out_shape=pltpu.HBM((per_dev, points, rhs), BF16),
        scratch_shapes=[
            pltpu.VMEM((rows + 1, rank, rhs), BF16),
            pltpu.VMEM((parents, rank, rhs), BF16),
            pltpu.VMEM(field.shape, BF16),
            pltpu.VMEM(joined.shape, BF16),
            pltpu.VMEM((per_dev, points, rhs), BF16),
            pltpu.SemaphoreType.DMA((2, chunks)),
            pltpu.SemaphoreType.DMA((chunks,)),
        ],
        compiler_params=params(32),
        cost_estimate=cost(6 * per_dev * points * rank * rhs, 24 * MIB),
        name="downward",
    )(sources, stacked, vmem(own), vmem(arrived), hbm(field), hbm(joined))


def side_by_side(coupling):
    width, rank, inner = coupling.shape
    return jnp.transpose(coupling, (1, 0, 2)).reshape(rank, width * inner)


def used_slots(sources, counts, zero_row):
    slots = lax.broadcasted_iota(jnp.int32, sources.shape[::-1], 0)
    return jnp.where(slots < counts[None, :], sources.T, zero_row)


def shards(
    charges,
    basis_in,
    basis_out,
    transfer,
    leaf_coupling,
    parent_coupling,
    leaf_sources,
    leaf_counts,
    leaf_sends,
    parent_sources,
    parent_counts,
    parent_sends,
):
    size = lax.axis_size("leaf")
    own = lax.axis_index("leaf").astype(jnp.int32).reshape(1)
    up = [(i, i + 1) for i in range(size - 1)]
    down = [(j, i) for i, j in up]
    up_leaf, low, high = leaf_coefficients(own, leaf_sends, charges, basis_in)
    from_left = lax.ppermute(high, "leaf", up)
    from_right = lax.ppermute(low, "leaf", down)
    up_parent, offered, joined = parent_coefficients(
        own, parent_sends, transfer, basis_out, up_leaf
    )
    arrived = lax.all_to_all(offered, "leaf", split_axis=0, concat_axis=0, tiled=True)
    leaf_rows = up_leaf.shape[0] + low.shape[0] + high.shape[0]
    field = leaf_lists(
        used_slots(leaf_sources, leaf_counts, leaf_rows),
        side_by_side(leaf_coupling),
        up_leaf,
        from_left,
        from_right,
    )
    return downward(
        used_slots(parent_sources, parent_counts, up_parent.shape[0] + offered.shape[0]),
        side_by_side(parent_coupling),
        up_parent,
        arrived,
        field,
        joined,
    )


def solution(mesh):
    return jax.shard_map(
        shards,
        mesh=mesh,
        in_specs=(
            P("leaf", None, None),
            P("leaf", None, None),
            P("leaf", None, None),
            P("leaf", None, None, None),
            P(),
            P(),
            P("leaf", None),
            P("leaf"),
            P(),
            P("leaf", None),
            P("leaf"),
            P(),
        ),
        out_specs=P("leaf", None, None),
        check_vma=False,
    )
```

```python
import jax
import jax.numpy as jnp
from jax import lax
from jax.experimental import pallas as pl
from jax.experimental.pallas import tpu as pltpu
from jax.sharding import PartitionSpec as P

MIB = 1 << 20
F32 = jnp.float32
BF16 = jnp.bfloat16

IN_VMEM = pl.BlockSpec(memory_space=pltpu.VMEM)
IN_SMEM = pl.BlockSpec(memory_space=pltpu.SMEM)
IN_HBM = pl.BlockSpec(memory_space=pltpu.HBM)


def params(mib):
    return pltpu.CompilerParams(vmem_limit_bytes=mib * MIB)


def cost(flops, moved):
    return pl.CostEstimate(flops=flops, bytes_accessed=moved, transcendentals=0)


def hbm(x):
    return pltpu.with_memory_space_constraint(x, pltpu.HBM)


def vmem(x):
    return pltpu.with_memory_space_constraint(x, pltpu.VMEM)


def first_rows_dot(a, b):
    return lax.dot_general(a, b, (((0,), (0,)), ((), ())), preferred_element_type=F32)


def leaves_kernel(
    own_ref, sends_ref, charges_hbm, basis_hbm, up_ref, far_hbm, near_hbm,
    charges, basis, offered, sends, sems, send_sem, out_sems,
):
    chunks = sems.shape[1]
    rows = charges.shape[0] // chunks

    def part(k, which):
        at = pl.ds(k * rows, rows)
        source, target = ((charges_hbm, charges), (basis_hbm, basis))[which]
        return pltpu.make_async_copy(source.at[at], target.at[at], sems.at[which, k])

    listing = pltpu.make_async_copy(sends_ref.at[own_ref[0]], sends, send_sem)
    for k in range(chunks):
        part(k, 0).start()
        part(k, 1).start()
    listing.start()
    for k in range(chunks):
        part(k, 0).wait()
        part(k, 1).wait()

        @pl.loop(0, rows // UP_LEAVES)
        def _(i):
            for c in range(UP_LEAVES):
                n = k * rows + UP_LEAVES * i + c
                up_ref[n] = jnp.dot(basis[n], charges[n], preferred_element_type=F32).astype(BF16)

    listing.wait()

    parts = out_sems.shape[1]
    count = offered.shape[1] // parts

    def result(which, k):
        at = pl.ds(k * count, count)
        target = (far_hbm, near_hbm)[which]
        return pltpu.make_async_copy(offered.at[which, at], target.at[at], out_sems.at[which, k])

    odd = lax.rem(own_ref[0], 2)
    for which, listed in enumerate((odd, 1 - odd)):
        for k in range(parts):

            @pl.loop(0, count // 16)
            def _(i):
                for c in range(16):
                    row = k * count + 16 * i + c
                    offered[which, row] = up_ref[sends[listed, row]]

            result(which, k).start()
    for which in range(2):
        for k in range(parts):
            result(which, k).wait()


UP_LEAVES = 32


def leaf_coefficients(own, leaf_sends, charges, basis_in):
    per_dev, points, rhs = charges.shape
    rank = basis_in.shape[1]
    side = leaf_sends.shape[2]
    chunks = 8
    return pl.pallas_call(
        leaves_kernel,
        in_specs=[IN_SMEM, IN_HBM, IN_HBM, IN_HBM],
        out_specs=[IN_VMEM, IN_HBM, IN_HBM],
        out_shape=[
            pltpu.VMEM((per_dev, rank, rhs), BF16),
            pltpu.HBM((side, rank, rhs), BF16),
            pltpu.HBM((side, rank, rhs), BF16),
        ],
        scratch_shapes=[
            pltpu.VMEM((per_dev, points, rhs), BF16),
            pltpu.VMEM((per_dev, rank, points), BF16),
            pltpu.VMEM((2, side, rank, rhs), BF16),
            pltpu.SMEM((2, side), jnp.int32),
            pltpu.SemaphoreType.DMA((2, chunks)),
            pltpu.SemaphoreType.DMA,
            pltpu.SemaphoreType.DMA((2, 2)),
        ],
        compiler_params=params(28),
        cost_estimate=cost(2 * per_dev * rank * points * rhs, 20 * MIB),
        name="leaf_coefficients",
    )(own, hbm(leaf_sends), hbm(charges), hbm(basis_in))


def parents_kernel(
    own_ref, sends_ref, transfer_hbm, leaf_ref, up_ref, offered_hbm,
    transfer, offered, sends, sems, send_sem, offer_sem,
):
    chunks = sems.shape[0]
    parents, _, rank, _ = transfer.shape
    rhs = leaf_ref.shape[2]
    rows = parents // chunks

    def part(k):
        at = pl.ds(k * rows, rows)
        return pltpu.make_async_copy(transfer_hbm.at[at], transfer.at[at], sems.at[k])

    own = own_ref[0]
    first = pl.multiple_of((own // 8) * 8, 8)
    listing = pltpu.make_async_copy(sends_ref.at[pl.ds(first, 8)], sends, send_sem)
    for k in range(chunks):
        part(k).start()
    listing.start()
    for k in range(chunks):
        part(k).wait()

        @pl.loop(0, rows // PARENTS)
        def _(i):
            for c in range(PARENTS):
                p = k * rows + PARENTS * i + c
                below = leaf_ref[pl.ds(8 * p, 8)].reshape(8 * rank, rhs)
                up_ref[p] = first_rows_dot(transfer[p].reshape(8 * rank, rank), below).astype(BF16)

    listing.wait()
    row = lax.rem(own, 8)

    @pl.loop(0, offered.shape[0] // 16)
    def _(i):
        for c in range(16):
            offered[16 * i + c] = up_ref[sends[row, 16 * i + c]]

    offer = pltpu.make_async_copy(offered, offered_hbm, offer_sem)
    offer.start()
    offer.wait()


PARENTS = 8


def parent_coefficients(own, parent_sends, transfer, up_leaf):
    parents, _, rank, _ = transfer.shape
    rhs = up_leaf.shape[2]
    count_dev = parent_sends.shape[0]
    chunks = 4
    return pl.pallas_call(
        parents_kernel,
        in_specs=[IN_SMEM, IN_HBM, IN_HBM, IN_VMEM],
        out_specs=[IN_VMEM, IN_HBM],
        out_shape=[
            pltpu.VMEM((parents, rank, rhs), BF16),
            pltpu.HBM((count_dev, rank, rhs), BF16),
        ],
        scratch_shapes=[
            pltpu.VMEM(transfer.shape, BF16),
            pltpu.VMEM((count_dev, rank, rhs), BF16),
            pltpu.SMEM((8, count_dev), jnp.int32),
            pltpu.SemaphoreType.DMA((chunks,)),
            pltpu.SemaphoreType.DMA,
            pltpu.SemaphoreType.DMA,
        ],
        compiler_params=params(16),
        cost_estimate=cost(16 * parents * rank * rank * rhs, 8 * MIB),
        name="parent_coefficients",
    )(own, hbm(parent_sends), hbm(transfer), vmem(up_leaf))


def joined_kernel(
    offered_hbm, transfer_hbm, basis_hbm, joined_hbm, same_hbm, transfer, basis, joined, sems, out_sems
):
    chunks = out_sems.shape[0]
    rows = transfer.shape[0] // chunks

    def part(k, which):
        if which:
            at = pl.ds(8 * k * rows, 8 * rows)
            return pltpu.make_async_copy(basis_hbm.at[at], basis.at[at], sems.at[1, k])
        at = pl.ds(k * rows, rows)
        return pltpu.make_async_copy(transfer_hbm.at[at], transfer.at[at], sems.at[0, k])

    def result(k):
        at = pl.ds(8 * k * rows, 8 * rows)
        return pltpu.make_async_copy(joined.at[at], joined_hbm.at[at], out_sems.at[k])

    for k in range(chunks):
        part(k, 0).start()
        part(k, 1).start()
    for k in range(chunks):
        part(k, 0).wait()
        part(k, 1).wait()

        @pl.loop(0, rows // JOINED)
        def _(i):
            for c in range(8 * JOINED):
                p = k * rows + JOINED * i + c // 8
                n = 8 * (k * rows + JOINED * i) + c
                pushed = first_rows_dot(transfer[p, c % 8], basis[n]).astype(BF16)
                joined[n] = jnp.concatenate([basis[n], pushed], axis=0).T

        result(k).start()
    for k in range(chunks):
        result(k).wait()


JOINED = 4


def joined_rows(offered, transfer, basis_out):
    parents, _, rank, _ = transfer.shape
    per_dev, _, points = basis_out.shape
    chunks = 4
    return pl.pallas_call(
        joined_kernel,
        in_specs=[IN_HBM, IN_HBM, IN_HBM],
        out_specs=[IN_HBM, IN_HBM],
        out_shape=[
            pltpu.HBM((per_dev, points, 2 * rank), BF16),
            pltpu.HBM(offered.shape, offered.dtype),
        ],
        input_output_aliases={0: 1},
        scratch_shapes=[
            pltpu.VMEM(transfer.shape, BF16),
            pltpu.VMEM(basis_out.shape, BF16),
            pltpu.VMEM((per_dev, points, 2 * rank), BF16),
            pltpu.SemaphoreType.DMA((2, chunks)),
            pltpu.SemaphoreType.DMA((chunks,)),
        ],
        compiler_params=params(28),
        cost_estimate=cost(2 * per_dev * points * rank * rank, 20 * MIB),
        name="joined_rows",
    )(hbm(offered), hbm(transfer), hbm(basis_out))


def list_fields(sources_ref, stacked, pool, first, count):
    width = sources_ref.shape[0]
    tiles = [
        jnp.concatenate([pool[sources_ref[j, first + q]] for j in range(width)], axis=0)
        for q in range(count)
    ]
    return jnp.dot(stacked, jnp.concatenate(tiles, axis=1), preferred_element_type=F32)


def fill(pool, *parts):
    for part, first in parts:

        @pl.loop(0, part.shape[0] // 8)
        def _(i):
            for c in range(8):
                pool[first + 8 * i + c] = part[8 * i + c]

    pool[pool.shape[0] - 1] = jnp.zeros(pool.shape[1:], pool.dtype)


def far_slots(far, is_far, rows_ref, slots_ref, keys_ref):
    width, targets = far.shape
    one = jnp.where(is_far, 1.0, 0.0)
    slot = lax.broadcasted_iota(jnp.int32, (width, targets), 0)
    earlier = lax.broadcasted_iota(jnp.int32, (width, width), 0) > lax.broadcasted_iota(
        jnp.int32, (width, width), 1
    )
    before = jnp.dot(
        jnp.where(earlier, 1.0, 0.0).astype(BF16), one.astype(BF16), preferred_element_type=F32
    ).astype(jnp.int32)
    for place in range(width):
        here = is_far & (before == place)
        slots_ref[place : place + 1] = jnp.min(
            jnp.where(here, slot, width), axis=0, keepdims=True
        )
        rows_ref[place : place + 1] = jnp.max(jnp.where(here, far, 0), axis=0, keepdims=True)
    used = jnp.sum(one, axis=0, keepdims=True)
    key = used * targets + lax.broadcasted_iota(jnp.int32, (1, targets), 1).astype(F32)
    across = jnp.broadcast_to(key, (targets, targets))
    down = across.T
    rank = jnp.sum(jnp.where(across > down, 1.0, 0.0), axis=1, keepdims=True).astype(jnp.int32)
    at = lax.broadcasted_iota(jnp.int32, (targets, targets), 1)
    keys = jnp.sum(jnp.where(rank == at, down, 0.0), axis=0, keepdims=True)
    keys_ref[...] = keys.astype(jnp.int32)


def lists_kernel(
    device_ref, early_ref, sources_ref, counts_ref, stacked_ref, own_hbm, near_ref,
    field_ref, rows_ref, slots_ref, keys_ref, pool, sem,
):
    own_rows, _, rhs = own_hbm.shape
    side = near_ref.shape[0]
    copy = pltpu.make_async_copy(own_hbm, pool.at[pl.ds(0, own_rows)], sem)
    copy.start()
    fill(pool, (near_ref, own_rows))
    sources = sources_ref[...]
    slot = lax.broadcasted_iota(jnp.int32, sources.shape, 0)
    far = sources - (own_rows + lax.rem(device_ref[0], 2) * side)
    is_far = (slot < counts_ref[...]) & (far >= 0) & (far < side)
    far_slots(far, is_far, rows_ref, slots_ref, keys_ref)
    copy.wait()

    @pl.loop(0, own_rows // LISTS)
    def _(i):
        lists = list_fields(early_ref, stacked_ref[...], pool, LISTS * i, LISTS)
        for q in range(LISTS):
            field_ref[LISTS * i + q] = lists[:, q * rhs : (q + 1) * rhs]


LISTS = 16


def leaf_lists(device, early, sources, counts, stacked, own, near):
    per_dev, rank, rhs = own.shape
    rows = own.shape[0] + near.shape[0]
    return pl.pallas_call(
        lists_kernel,
        in_specs=[IN_SMEM, IN_SMEM, IN_VMEM, IN_VMEM, IN_VMEM, IN_HBM, IN_VMEM],
        out_specs=[IN_VMEM] * 4,
        out_shape=[
            pltpu.VMEM((per_dev, rank, rhs), F32),
            jax.ShapeDtypeStruct(sources.shape, jnp.int32),
            jax.ShapeDtypeStruct(sources.shape, jnp.int32),
            jax.ShapeDtypeStruct((1, per_dev), jnp.int32),
        ],
        scratch_shapes=[
            pltpu.VMEM((rows + 1, rank, rhs), BF16),
            pltpu.SemaphoreType.DMA,
        ],
        compiler_params=params(32),
        cost_estimate=cost(2 * per_dev * sources.shape[0] * rank * rank * rhs, 12 * MIB),
        name="leaf_lists",
    )(device, early, sources, counts, stacked, hbm(own), vmem(near))


def far_kernel(
    keys_ref, rows_ref, slots_ref, wide_ref, far_ref, partial_ref, field_hbm, total, field, sem
):
    block = total.shape[0]
    per_dev = field.shape[0]

    def products(t, g):
        blocks = [
            wide_ref[0, slots_ref[4 * g + i, t]] + wide_ref[1, slots_ref[4 * g + i + 1, t]]
            for i in (0, 2)
        ]
        tiles = [far_ref[rows_ref[4 * g + i, t]] for i in range(4)]
        return jnp.dot(
            jnp.concatenate(blocks, axis=1),
            jnp.concatenate(tiles, axis=0),
            preferred_element_type=F32,
        )

    @pl.loop(0, per_dev // block)
    def _(b):
        targets = [lax.rem(keys_ref[0, block * b + q], per_dev) for q in range(block)]
        most = lax.div(keys_ref[0, block * b], per_dev)

        for q, t in enumerate(targets):
            total[q] = partial_ref[t] + products(t, 0)

        @pl.loop(1, lax.div(most + 3, 4))
        def _(g):
            for q, t in enumerate(targets):
                total[q] += products(t, g)

        for q, t in enumerate(targets):
            field[t] = total[q].astype(BF16)
            pltpu.make_async_copy(field.at[t], field_hbm.at[t], sem).start()

    pltpu.make_async_copy(field, field_hbm, sem).wait()


FAR = 32


def far_lists(keys, rows, slots, wide, far, partial):
    per_dev, rank, rhs = partial.shape
    return pl.pallas_call(
        far_kernel,
        in_specs=[IN_SMEM, IN_SMEM, IN_SMEM, IN_VMEM, IN_VMEM, IN_VMEM],
        out_specs=IN_HBM,
        out_shape=pltpu.HBM((per_dev, rank, rhs), BF16),
        scratch_shapes=[
            pltpu.VMEM((FAR, rank, rhs), F32),
            pltpu.VMEM((per_dev, rank, rhs), BF16),
            pltpu.SemaphoreType.DMA,
        ],
        compiler_params=params(24),
        cost_estimate=cost(8 * per_dev * rank * rank * rhs, 20 * MIB),
        name="far_lists",
    )(keys, rows, slots, wide, vmem(far), vmem(partial))


def down_kernel(
    sources_ref, stacked_ref, own_ref, arrived_ref, field_hbm, joined_hbm, potential_hbm,
    pool, down, field, joined, potential, sems, out_sems,
):
    chunks = out_sems.shape[0]
    parents, _, rhs = own_ref.shape
    rows = joined.shape[0] // chunks

    def part(k, which):
        at = pl.ds(k * rows, rows)
        source, target = ((field_hbm, field), (joined_hbm, joined))[which]
        return pltpu.make_async_copy(source.at[at], target.at[at], sems.at[which, k])

    def result(k):
        at = pl.ds(k * rows, rows)
        return pltpu.make_async_copy(potential.at[at], potential_hbm.at[at], out_sems.at[k])

    for k in range(chunks):
        part(k, 0).start()
        part(k, 1).start()
    fill(pool, (own_ref, 0), (arrived_ref, parents))

    @pl.loop(0, parents // DOWN_LISTS)
    def _(i):
        lists = list_fields(sources_ref, stacked_ref[...], pool, DOWN_LISTS * i, DOWN_LISTS)
        for q in range(DOWN_LISTS):
            down[DOWN_LISTS * i + q] = lists[:, q * rhs : (q + 1) * rhs].astype(BF16)

    for k in range(chunks):
        part(k, 0).wait()
        part(k, 1).wait()

        @pl.loop(0, rows // (8 * DOWN_PARENTS))
        def _(i):
            for q in range(DOWN_PARENTS):
                p = k * (rows // 8) + DOWN_PARENTS * i + q
                for c in range(8):
                    n = 8 * p + c
                    both = jnp.concatenate([field[n], down[p]], axis=0)
                    potential[n] = jnp.dot(joined[n], both, preferred_element_type=F32).astype(BF16)

        result(k).start()
    for k in range(chunks):
        result(k).wait()


DOWN_LISTS = 4
DOWN_PARENTS = 4
DOWN_CHUNKS = 8


def downward(sources, stacked, own, arrived, field, joined):
    parents, rank, rhs = own.shape
    per_dev, points, _ = joined.shape
    rows = own.shape[0] + arrived.shape[0]
    chunks = DOWN_CHUNKS
    return pl.pallas_call(
        down_kernel,
        in_specs=[IN_SMEM, IN_VMEM, IN_VMEM, IN_VMEM, IN_HBM, IN_HBM],
        out_specs=IN_HBM,
        out_shape=pltpu.HBM((per_dev, points, rhs), BF16),
        scratch_shapes=[
            pltpu.VMEM((rows + 1, rank, rhs), BF16),
            pltpu.VMEM((parents, rank, rhs), BF16),
            pltpu.VMEM(field.shape, BF16),
            pltpu.VMEM(joined.shape, BF16),
            pltpu.VMEM((per_dev, points, rhs), BF16),
            pltpu.SemaphoreType.DMA((2, chunks)),
            pltpu.SemaphoreType.DMA((chunks,)),
        ],
        compiler_params=params(40),
        cost_estimate=cost(6 * per_dev * points * rank * rhs, 24 * MIB),
        name="downward",
    )(sources, stacked, vmem(own), vmem(arrived), hbm(field), hbm(joined))


def side_by_side(coupling):
    width, rank, inner = coupling.shape
    return jnp.transpose(coupling, (1, 0, 2)).reshape(rank, width * inner)


def both_halves(coupling):
    inner = coupling.shape[2]
    blocks = jnp.pad(coupling, ((0, 1), (0, 0), (0, 0)))
    return jnp.stack(
        [
            jnp.pad(blocks, ((0, 0), (0, 0), (0, inner))),
            jnp.pad(blocks, ((0, 0), (0, 0), (inner, 0))),
        ]
    )


def used_slots(sources, counts, zero_row):
    slots = lax.broadcasted_iota(jnp.int32, sources.shape[::-1], 0)
    return jnp.where(slots < counts[None, :], sources.T, zero_row)


def shards(
    charges,
    basis_in,
    basis_out,
    transfer,
    leaf_coupling,
    parent_coupling,
    leaf_sources,
    leaf_counts,
    leaf_sends,
    parent_sources,
    parent_counts,
    parent_sends,
):
    size = lax.axis_size("leaf")
    own = lax.axis_index("leaf").astype(jnp.int32).reshape(1)
    on_chip = [(i, i ^ 1) for i in range(size)]
    off_chip = [(i, i + 1) for i in range(1, size - 1, 2)]
    off_chip += [(j, i) for i, j in off_chip]
    up_leaf, far, near = leaf_coefficients(own, leaf_sends, charges, basis_in)
    from_far = lax.ppermute(far, "leaf", off_chip)
    from_near = lax.ppermute(near, "leaf", on_chip)
    up_parent, offered = parent_coefficients(own, parent_sends, transfer, up_leaf)
    joined, offered = joined_rows(offered, transfer, basis_out)
    arrived = lax.all_to_all(offered, "leaf", split_axis=0, concat_axis=0, tiled=True)
    own_rows, side = up_leaf.shape[0], far.shape[0]
    odd = own[0] % 2
    far_first = own_rows + odd * side
    near_first = own_rows + (1 - odd) * side
    sources = leaf_sources.T
    used = lax.broadcasted_iota(jnp.int32, sources.shape, 0) < leaf_counts[None, :]
    is_far = used & (sources >= far_first) & (sources < far_first + side)
    is_near = sources >= own_rows
    early = jnp.where(is_near, sources - near_first + own_rows, sources)
    early = jnp.where(used & ~is_far, early, own_rows + side)
    partial, far_rows, slots, keys = leaf_lists(
        own, early, sources, leaf_counts[None, :], side_by_side(leaf_coupling), up_leaf, from_near
    )
    field = far_lists(keys, far_rows, slots, both_halves(leaf_coupling), from_far, partial)
    return downward(
        used_slots(parent_sources, parent_counts, up_parent.shape[0] + offered.shape[0]),
        side_by_side(parent_coupling),
        up_parent,
        arrived,
        field,
        joined,
    )


def solution(mesh):
    return jax.shard_map(
        shards,
        mesh=mesh,
        in_specs=(
            P("leaf", None, None),
            P("leaf", None, None),
            P("leaf", None, None),
            P("leaf", None, None, None),
            P(),
            P(),
            P("leaf", None),
            P("leaf"),
            P(),
            P("leaf", None),
            P("leaf"),
            P(),
        ),
        out_specs=P("leaf", None, None),
        check_vma=False,
    )
```

```python
import jax
import jax.numpy as jnp
from jax import lax
from jax.experimental import pallas as pl
from jax.experimental.pallas import tpu as pltpu
from jax.sharding import PartitionSpec as P

MIB = 1 << 20
F32 = jnp.float32
BF16 = jnp.bfloat16

IN_VMEM = pl.BlockSpec(memory_space=pltpu.VMEM)
IN_SMEM = pl.BlockSpec(memory_space=pltpu.SMEM)
IN_HBM = pl.BlockSpec(memory_space=pltpu.HBM)


def params(mib):
    return pltpu.CompilerParams(vmem_limit_bytes=mib * MIB)


def cost(flops, moved):
    return pl.CostEstimate(flops=flops, bytes_accessed=moved, transcendentals=0)


def hbm(x):
    return pltpu.with_memory_space_constraint(x, pltpu.HBM)


def vmem(x):
    return pltpu.with_memory_space_constraint(x, pltpu.VMEM)


def first_rows_dot(a, b):
    return lax.dot_general(a, b, (((0,), (0,)), ((), ())), preferred_element_type=F32)


def leaves_kernel(
    own_ref, sends_ref, charges_hbm, basis_hbm, up_ref, far_hbm, near_hbm,
    charges, basis, offered, sends, sems, send_sem, out_sems,
):
    chunks = sems.shape[1]
    rows = charges.shape[0] // chunks

    def part(k, which):
        at = pl.ds(k * rows, rows)
        source, target = ((charges_hbm, charges), (basis_hbm, basis))[which]
        return pltpu.make_async_copy(source.at[at], target.at[at], sems.at[which, k])

    listing = pltpu.make_async_copy(sends_ref.at[own_ref[0]], sends, send_sem)
    for k in range(chunks):
        part(k, 0).start()
        part(k, 1).start()
    listing.start()
    for k in range(chunks):
        part(k, 0).wait()
        part(k, 1).wait()

        @pl.loop(0, rows // UP_LEAVES)
        def _(i):
            for c in range(UP_LEAVES):
                n = k * rows + UP_LEAVES * i + c
                up_ref[n] = jnp.dot(basis[n], charges[n], preferred_element_type=F32).astype(BF16)

    listing.wait()

    parts = out_sems.shape[1]
    count = offered.shape[1] // parts

    def result(which, k):
        at = pl.ds(k * count, count)
        target = (far_hbm, near_hbm)[which]
        return pltpu.make_async_copy(offered.at[which, at], target.at[at], out_sems.at[which, k])

    odd = lax.rem(own_ref[0], 2)
    for which, listed in enumerate((odd, 1 - odd)):
        for k in range(parts):

            @pl.loop(0, count // 16)
            def _(i):
                for c in range(16):
                    row = k * count + 16 * i + c
                    offered[which, row] = up_ref[sends[listed, row]]

            result(which, k).start()
    for which in range(2):
        for k in range(parts):
            result(which, k).wait()


UP_LEAVES = 32


def leaf_coefficients(own, leaf_sends, charges, basis_in):
    per_dev, points, rhs = charges.shape
    rank = basis_in.shape[1]
    side = leaf_sends.shape[2]
    chunks = 8
    return pl.pallas_call(
        leaves_kernel,
        in_specs=[IN_SMEM, IN_HBM, IN_HBM, IN_HBM],
        out_specs=[IN_VMEM, IN_HBM, IN_HBM],
        out_shape=[
            pltpu.VMEM((per_dev, rank, rhs), BF16),
            pltpu.HBM((side, rank, rhs), BF16),
            pltpu.HBM((side, rank, rhs), BF16),
        ],
        scratch_shapes=[
            pltpu.VMEM((per_dev, points, rhs), BF16),
            pltpu.VMEM((per_dev, rank, points), BF16),
            pltpu.VMEM((2, side, rank, rhs), BF16),
            pltpu.SMEM((2, side), jnp.int32),
            pltpu.SemaphoreType.DMA((2, chunks)),
            pltpu.SemaphoreType.DMA,
            pltpu.SemaphoreType.DMA((2, 2)),
        ],
        compiler_params=params(28),
        cost_estimate=cost(2 * per_dev * rank * points * rhs, 20 * MIB),
        name="leaf_coefficients",
    )(own, hbm(leaf_sends), hbm(charges), hbm(basis_in))


def parents_kernel(
    own_ref, sends_ref, transfer_hbm, leaf_ref, up_ref, offered_hbm,
    transfer, offered, sends, sems, send_sem, offer_sem,
):
    chunks = sems.shape[0]
    parents, _, rank, _ = transfer.shape
    rhs = leaf_ref.shape[2]
    rows = parents // chunks

    def part(k):
        at = pl.ds(k * rows, rows)
        return pltpu.make_async_copy(transfer_hbm.at[at], transfer.at[at], sems.at[k])

    own = own_ref[0]
    first = pl.multiple_of((own // 8) * 8, 8)
    listing = pltpu.make_async_copy(sends_ref.at[pl.ds(first, 8)], sends, send_sem)
    for k in range(chunks):
        part(k).start()
    listing.start()
    for k in range(chunks):
        part(k).wait()

        @pl.loop(0, rows // PARENTS)
        def _(i):
            for c in range(PARENTS):
                p = k * rows + PARENTS * i + c
                below = leaf_ref[pl.ds(8 * p, 8)].reshape(8 * rank, rhs)
                up_ref[p] = first_rows_dot(transfer[p].reshape(8 * rank, rank), below).astype(BF16)

    listing.wait()
    row = lax.rem(own, 8)

    @pl.loop(0, offered.shape[0] // 16)
    def _(i):
        for c in range(16):
            offered[16 * i + c] = up_ref[sends[row, 16 * i + c]]

    offer = pltpu.make_async_copy(offered, offered_hbm, offer_sem)
    offer.start()
    offer.wait()


PARENTS = 8


def parent_coefficients(own, parent_sends, transfer, up_leaf):
    parents, _, rank, _ = transfer.shape
    rhs = up_leaf.shape[2]
    count_dev = parent_sends.shape[0]
    chunks = 4
    return pl.pallas_call(
        parents_kernel,
        in_specs=[IN_SMEM, IN_HBM, IN_HBM, IN_VMEM],
        out_specs=[IN_VMEM, IN_HBM],
        out_shape=[
            pltpu.VMEM((parents, rank, rhs), BF16),
            pltpu.HBM((count_dev, rank, rhs), BF16),
        ],
        scratch_shapes=[
            pltpu.VMEM(transfer.shape, BF16),
            pltpu.VMEM((count_dev, rank, rhs), BF16),
            pltpu.SMEM((8, count_dev), jnp.int32),
            pltpu.SemaphoreType.DMA((chunks,)),
            pltpu.SemaphoreType.DMA,
            pltpu.SemaphoreType.DMA,
        ],
        compiler_params=params(16),
        cost_estimate=cost(16 * parents * rank * rank * rhs, 8 * MIB),
        name="parent_coefficients",
    )(own, hbm(parent_sends), hbm(transfer), vmem(up_leaf))


def joined_kernel(
    offered_hbm, transfer_hbm, basis_hbm, joined_hbm, same_hbm, transfer, basis, joined, sems, out_sems
):
    chunks = out_sems.shape[0]
    rows = transfer.shape[0] // chunks

    def part(k, which):
        if which:
            at = pl.ds(8 * k * rows, 8 * rows)
            return pltpu.make_async_copy(basis_hbm.at[at], basis.at[at], sems.at[1, k])
        at = pl.ds(k * rows, rows)
        return pltpu.make_async_copy(transfer_hbm.at[at], transfer.at[at], sems.at[0, k])

    def result(k):
        at = pl.ds(8 * k * rows, 8 * rows)
        return pltpu.make_async_copy(joined.at[at], joined_hbm.at[at], out_sems.at[k])

    for k in range(chunks):
        part(k, 0).start()
        part(k, 1).start()
    for k in range(chunks):
        part(k, 0).wait()
        part(k, 1).wait()

        @pl.loop(0, rows // JOINED)
        def _(i):
            for c in range(8 * JOINED):
                p = k * rows + JOINED * i + c // 8
                n = 8 * (k * rows + JOINED * i) + c
                pushed = first_rows_dot(transfer[p, c % 8], basis[n]).astype(BF16)
                joined[n] = jnp.concatenate([basis[n], pushed], axis=0).T

        result(k).start()
    for k in range(chunks):
        result(k).wait()


JOINED = 4


def joined_rows(offered, transfer, basis_out):
    parents, _, rank, _ = transfer.shape
    per_dev, _, points = basis_out.shape
    chunks = 4
    return pl.pallas_call(
        joined_kernel,
        in_specs=[IN_HBM, IN_HBM, IN_HBM],
        out_specs=[IN_HBM, IN_HBM],
        out_shape=[
            pltpu.HBM((per_dev, points, 2 * rank), BF16),
            pltpu.HBM(offered.shape, offered.dtype),
        ],
        input_output_aliases={0: 1},
        scratch_shapes=[
            pltpu.VMEM(transfer.shape, BF16),
            pltpu.VMEM(basis_out.shape, BF16),
            pltpu.VMEM((per_dev, points, 2 * rank), BF16),
            pltpu.SemaphoreType.DMA((2, chunks)),
            pltpu.SemaphoreType.DMA((chunks,)),
        ],
        compiler_params=params(28),
        cost_estimate=cost(2 * per_dev * points * rank * rank, 20 * MIB),
        name="joined_rows",
    )(hbm(offered), hbm(transfer), hbm(basis_out))


def list_fields(sources_ref, stacked, pool, first, count):
    width = sources_ref.shape[0]
    tiles = [
        jnp.concatenate([pool[sources_ref[j, first + q]] for j in range(width)], axis=0)
        for q in range(count)
    ]
    return jnp.dot(stacked, jnp.concatenate(tiles, axis=1), preferred_element_type=F32)


def fill(pool, *parts):
    for part, first in parts:

        @pl.loop(0, part.shape[0] // 8)
        def _(i):
            for c in range(8):
                pool[first + 8 * i + c] = part[8 * i + c]

    pool[pool.shape[0] - 1] = jnp.zeros(pool.shape[1:], pool.dtype)


def far_slots(far, is_far, rows_ref, slots_ref, keys_ref):
    width, targets = far.shape
    one = jnp.where(is_far, 1.0, 0.0)
    slot = lax.broadcasted_iota(jnp.int32, (width, targets), 0)
    earlier = lax.broadcasted_iota(jnp.int32, (width, width), 0) > lax.broadcasted_iota(
        jnp.int32, (width, width), 1
    )
    before = jnp.dot(
        jnp.where(earlier, 1.0, 0.0).astype(BF16), one.astype(BF16), preferred_element_type=F32
    ).astype(jnp.int32)
    for place in range(width):
        here = is_far & (before == place)
        slots_ref[place : place + 1] = jnp.min(
            jnp.where(here, slot, width), axis=0, keepdims=True
        )
        rows_ref[place : place + 1] = jnp.max(jnp.where(here, far, 0), axis=0, keepdims=True)
    used = jnp.sum(one, axis=0, keepdims=True)
    key = used * targets + lax.broadcasted_iota(jnp.int32, (1, targets), 1).astype(F32)
    across = jnp.broadcast_to(key, (targets, targets))
    down = across.T
    rank = jnp.sum(jnp.where(across > down, 1.0, 0.0), axis=1, keepdims=True).astype(jnp.int32)
    at = lax.broadcasted_iota(jnp.int32, (targets, targets), 1)
    keys = jnp.sum(jnp.where(rank == at, down, 0.0), axis=0, keepdims=True)
    keys_ref[...] = keys.astype(jnp.int32)


def lists_kernel(
    device_ref, early_ref, sources_ref, counts_ref, stacked_ref, own_hbm, near_ref,
    field_ref, rows_ref, slots_ref, keys_ref, pool, sem,
):
    own_rows, _, rhs = own_hbm.shape
    side = near_ref.shape[0]
    copy = pltpu.make_async_copy(own_hbm, pool.at[pl.ds(0, own_rows)], sem)
    copy.start()
    fill(pool, (near_ref, own_rows))
    sources = sources_ref[...]
    slot = lax.broadcasted_iota(jnp.int32, sources.shape, 0)
    far = sources - (own_rows + lax.rem(device_ref[0], 2) * side)
    is_far = (slot < counts_ref[...]) & (far >= 0) & (far < side)
    far_slots(far, is_far, rows_ref, slots_ref, keys_ref)
    copy.wait()

    @pl.loop(0, own_rows // LISTS)
    def _(i):
        lists = list_fields(early_ref, stacked_ref[...], pool, LISTS * i, LISTS)
        for q in range(LISTS):
            field_ref[LISTS * i + q] = lists[:, q * rhs : (q + 1) * rhs]


LISTS = 16


def leaf_lists(device, early, sources, counts, stacked, own, near):
    per_dev, rank, rhs = own.shape
    rows = own.shape[0] + near.shape[0]
    return pl.pallas_call(
        lists_kernel,
        in_specs=[IN_SMEM, IN_SMEM, IN_VMEM, IN_VMEM, IN_VMEM, IN_HBM, IN_VMEM],
        out_specs=[IN_VMEM] * 4,
        out_shape=[
            pltpu.VMEM((per_dev, rank, rhs), F32),
            jax.ShapeDtypeStruct(sources.shape, jnp.int32),
            jax.ShapeDtypeStruct(sources.shape, jnp.int32),
            jax.ShapeDtypeStruct((1, per_dev), jnp.int32),
        ],
        scratch_shapes=[
            pltpu.VMEM((rows + 1, rank, rhs), BF16),
            pltpu.SemaphoreType.DMA,
        ],
        compiler_params=params(32),
        cost_estimate=cost(2 * per_dev * sources.shape[0] * rank * rank * rhs, 12 * MIB),
        name="leaf_lists",
    )(device, early, sources, counts, stacked, hbm(own), vmem(near))


def far_kernel(
    keys_ref, rows_ref, slots_ref, wide_ref, far_ref, partial_ref, field_hbm, total, field, sem
):
    block = total.shape[0]
    per_dev = field.shape[0]

    def products(t, g):
        blocks = [
            wide_ref[0, slots_ref[4 * g + i, t]] + wide_ref[1, slots_ref[4 * g + i + 1, t]]
            for i in (0, 2)
        ]
        tiles = [far_ref[rows_ref[4 * g + i, t]] for i in range(4)]
        return jnp.dot(
            jnp.concatenate(blocks, axis=1),
            jnp.concatenate(tiles, axis=0),
            preferred_element_type=F32,
        )

    @pl.loop(0, per_dev // block)
    def _(b):
        targets = [lax.rem(keys_ref[0, block * b + q], per_dev) for q in range(block)]
        most = lax.div(keys_ref[0, block * b], per_dev)

        for q, t in enumerate(targets):
            total[q] = partial_ref[t] + products(t, 0)

        @pl.loop(1, lax.div(most + 3, 4))
        def _(g):
            for q, t in enumerate(targets):
                total[q] += products(t, g)

        for q, t in enumerate(targets):
            field[t] = total[q].astype(BF16)
            pltpu.make_async_copy(field.at[t], field_hbm.at[t], sem).start()

    pltpu.make_async_copy(field, field_hbm, sem).wait()


FAR = 32


def far_lists(keys, rows, slots, wide, far, partial):
    per_dev, rank, rhs = partial.shape
    return pl.pallas_call(
        far_kernel,
        in_specs=[IN_SMEM, IN_SMEM, IN_SMEM, IN_VMEM, IN_VMEM, IN_VMEM],
        out_specs=IN_HBM,
        out_shape=pltpu.HBM((per_dev, rank, rhs), BF16),
        scratch_shapes=[
            pltpu.VMEM((FAR, rank, rhs), F32),
            pltpu.VMEM((per_dev, rank, rhs), BF16),
            pltpu.SemaphoreType.DMA,
        ],
        compiler_params=params(24),
        cost_estimate=cost(8 * per_dev * rank * rank * rhs, 20 * MIB),
        name="far_lists",
    )(keys, rows, slots, wide, vmem(far), vmem(partial))


def down_kernel(
    sources_ref, stacked_ref, own_ref, arrived_ref, field_hbm, joined_hbm, potential_hbm,
    pool, down, field, joined, potential, sems, out_sems,
):
    chunks = out_sems.shape[0]
    parents, _, rhs = own_ref.shape
    rows = joined.shape[0] // chunks

    def part(k, which):
        at = pl.ds(k * rows, rows)
        source, target = ((field_hbm, field), (joined_hbm, joined))[which]
        return pltpu.make_async_copy(source.at[at], target.at[at], sems.at[which, k])

    def result(k):
        at = pl.ds(k * rows, rows)
        return pltpu.make_async_copy(potential.at[at], potential_hbm.at[at], out_sems.at[k])

    for k in range(chunks):
        part(k, 0).start()
        part(k, 1).start()
    fill(pool, (own_ref, 0), (arrived_ref, parents))

    @pl.loop(0, parents // DOWN_LISTS)
    def _(i):
        lists = list_fields(sources_ref, stacked_ref[...], pool, DOWN_LISTS * i, DOWN_LISTS)
        for q in range(DOWN_LISTS):
            down[DOWN_LISTS * i + q] = lists[:, q * rhs : (q + 1) * rhs].astype(BF16)

    for k in range(chunks):
        part(k, 0).wait()
        part(k, 1).wait()

        @pl.loop(0, rows // (8 * DOWN_PARENTS))
        def _(i):
            for q in range(DOWN_PARENTS):
                p = k * (rows // 8) + DOWN_PARENTS * i + q
                for c in range(8):
                    n = 8 * p + c
                    both = jnp.concatenate([field[n], down[p]], axis=0)
                    potential[n] = jnp.dot(joined[n], both, preferred_element_type=F32).astype(BF16)

        result(k).start()
    for k in range(chunks):
        result(k).wait()


DOWN_LISTS = 4
DOWN_PARENTS = 4
DOWN_CHUNKS = 8


def downward(sources, stacked, own, arrived, field, joined):
    parents, rank, rhs = own.shape
    per_dev, points, _ = joined.shape
    rows = own.shape[0] + arrived.shape[0]
    chunks = DOWN_CHUNKS
    return pl.pallas_call(
        down_kernel,
        in_specs=[IN_SMEM, IN_VMEM, IN_VMEM, IN_VMEM, IN_HBM, IN_HBM],
        out_specs=IN_HBM,
        out_shape=pltpu.HBM((per_dev, points, rhs), BF16),
        scratch_shapes=[
            pltpu.VMEM((rows + 1, rank, rhs), BF16),
            pltpu.VMEM((parents, rank, rhs), BF16),
            pltpu.VMEM(field.shape, BF16),
            pltpu.VMEM(joined.shape, BF16),
            pltpu.VMEM((per_dev, points, rhs), BF16),
            pltpu.SemaphoreType.DMA((2, chunks)),
            pltpu.SemaphoreType.DMA((chunks,)),
        ],
        compiler_params=params(40),
        cost_estimate=cost(6 * per_dev * points * rank * rhs, 24 * MIB),
        name="downward",
    )(sources, stacked, vmem(own), vmem(arrived), hbm(field), hbm(joined))


def side_by_side(coupling):
    width, rank, inner = coupling.shape
    return jnp.transpose(coupling, (1, 0, 2)).reshape(rank, width * inner)


def both_halves(coupling):
    inner = coupling.shape[2]
    blocks = jnp.pad(coupling, ((0, 1), (0, 0), (0, 0)))
    return jnp.stack(
        [
            jnp.pad(blocks, ((0, 0), (0, 0), (0, inner))),
            jnp.pad(blocks, ((0, 0), (0, 0), (inner, 0))),
        ]
    )


def used_slots(sources, counts, zero_row):
    slots = lax.broadcasted_iota(jnp.int32, sources.shape[::-1], 0)
    return jnp.where(slots < counts[None, :], sources.T, zero_row)


def shards(
    charges,
    basis_in,
    basis_out,
    transfer,
    leaf_coupling,
    parent_coupling,
    leaf_sources,
    leaf_counts,
    leaf_sends,
    parent_sources,
    parent_counts,
    parent_sends,
):
    size = lax.axis_size("leaf")
    own = lax.axis_index("leaf").astype(jnp.int32).reshape(1)
    on_chip = [(i, i ^ 1) for i in range(size)]
    off_chip = [(i, i + 1) for i in range(1, size - 1, 2)]
    off_chip += [(j, i) for i, j in off_chip]
    up_leaf, far, near = leaf_coefficients(own, leaf_sends, charges, basis_in)
    from_near = lax.ppermute(near, "leaf", on_chip)
    from_far = lax.ppermute(far, "leaf", off_chip)
    up_parent, offered = parent_coefficients(own, parent_sends, transfer, up_leaf)
    joined, offered = joined_rows(offered, transfer, basis_out)
    arrived = lax.all_to_all(offered, "leaf", split_axis=0, concat_axis=0, tiled=True)
    own_rows, side = up_leaf.shape[0], far.shape[0]
    odd = own[0] % 2
    far_first = own_rows + odd * side
    near_first = own_rows + (1 - odd) * side
    sources = leaf_sources.T
    used = lax.broadcasted_iota(jnp.int32, sources.shape, 0) < leaf_counts[None, :]
    is_far = used & (sources >= far_first) & (sources < far_first + side)
    is_near = sources >= own_rows
    early = jnp.where(is_near, sources - near_first + own_rows, sources)
    early = jnp.where(used & ~is_far, early, own_rows + side)
    partial, far_rows, slots, keys = leaf_lists(
        own, early, sources, leaf_counts[None, :], side_by_side(leaf_coupling), up_leaf, from_near
    )
    field = far_lists(keys, far_rows, slots, both_halves(leaf_coupling), from_far, partial)
    return downward(
        used_slots(parent_sources, parent_counts, up_parent.shape[0] + offered.shape[0]),
        side_by_side(parent_coupling),
        up_parent,
        arrived,
        field,
        joined,
    )


def solution(mesh):
    return jax.shard_map(
        shards,
        mesh=mesh,
        in_specs=(
            P("leaf", None, None),
            P("leaf", None, None),
            P("leaf", None, None),
            P("leaf", None, None, None),
            P(),
            P(),
            P("leaf", None),
            P("leaf"),
            P(),
            P("leaf", None),
            P("leaf"),
            P(),
        ),
        out_specs=P("leaf", None, None),
        check_vma=False,
    )
```
